32 devices in a mesh: parts: 2 (over y), ctx: 4 (over z), head: 4 (over x, core).
Axes of the slice: x: 2, y: 2, z: 4, core: 2. Of those that a mesh axis runs over, the one named last changes fastest.
Arguments:
- event_ids: int32 [8192], P(('parts', 'ctx')), parts along dimension 0, may hold values from 0 to 255
- embed_table: bfloat16 [256, 1024], replicated, may hold values from -6 to 6
- w_qkv: bfloat16 [1024, 3072], P(None, 'head'), may hold values from -0.1875 to 0.1875
- norm_gain: float32 [1024], P('head'), may hold values from 0.1 to 1.9
- w_out: bfloat16 [1024, 1024], P('head'), may hold values from -0.1875 to 0.1875
- init_state: float32 [8, 128, 128], P('head'), may hold values from -6 to 6
- out_grad: bfloat16 [8192, 1024], P(('parts', 'ctx')), parts along dimension 0, may hold values from -1 to 1
Outputs:
- layer_out: bfloat16 [8192, 1024], P(('parts', 'ctx'), 'head'), parts along dimension 0
- grad_wqkv: float32 [2048, 3072], P(('parts', 'ctx'), 'head'), parts along dimension 0
- grad_wout: float32 [2048, 1024], P(('parts', 'head'), 'ctx'), parts along dimension 0
- grad_gain: float32 [2048], P(('parts', 'head')), parts along dimension 0
- grad_init: float32 [16, 128, 128], P(('parts', 'head')), parts along dimension 0
- grad_table: float32 [512, 1024], P('parts'), parts along dimension 0
The draws below stay inside these ranges and needn't reach their ends.
There are 2 independent parts, one for each index of `parts`. The reference program is written for one: setup_inputs(seed, part) draws one part's arguments, and reference() takes and returns one part's arrays. A program takes and returns all parts, laid end to end along the dimension named above; an argument that names none is the same for every part. Nothing has to cross between parts.
All inputs are finite; a program needn't handle non-finite values.
Results may differ from the reference program's by a relative error of at most 0.0082.
Values sent between devices are 32-bit elements; how exact they have to be, the bound alone decides.
A program may use at most 64 MiB of HBM per device.

```python
import math
import jax
import jax.numpy as jnp
import numpy as np
from jax import lax

D = 1024
H = 8
DH = 128
V = 256
BLOCK = 128
TOKENS = 4096


def place_ends(entries, key, least, top_value):
    extent = entries.shape
    index_at = [jax.random.randint(jax.random.fold_in(key, axis), (), 0, extent[axis]) for axis in range(len(extent))]
    entries = entries.at[tuple(index_at)].set(least)
    longest = extent.index(max(extent))
    index_at[longest] = (index_at[longest] + 1) % extent[longest]
    return entries.at[tuple(index_at)].set(top_value)


def level_of(own_key, dims, cuts, low, high):
    def one(position, blocks):
        heights = jax.random.uniform(jax.random.fold_in(jax.random.fold_in(own_key, 6), position), (blocks,), jnp.float32, low / len(cuts), high / len(cuts))
        return jnp.repeat(jnp.exp(heights), dims[position] // blocks).reshape((-1,) + (1,) * (len(dims) - position - 1))

    level = one(*cuts[0])
    for cut in cuts[1:]:
        level = level * one(*cut)
    return level


def rank_bounds(count, slope):
    weights = [(1 << 20) // math.isqrt(grade ** slope) + 1 for grade in range(1, count + 1)]
    scale = 1 + sum(weights) // (1 << 30)
    return np.cumsum(np.array([max(1, weight // scale) for weight in weights]))


def skewed_ids(own_key, dims, count, lean):
    table = rank_bounds(count, lean)
    ticket = jax.random.randint(jax.random.fold_in(own_key, 1), dims, 0, int(table[count - 1]))
    grade = jnp.searchsorted(jnp.asarray(table, jnp.int32), ticket, side="right")
    return jax.random.permutation(jax.random.fold_in(own_key, 2), count)[grade].astype(jnp.int32)


def normal_values(own_key, dims, scale, most, shards=(), kind=jnp.bfloat16):
    level = level_of(own_key, dims, shards, -0.22, 0.18) if shards else 1.0
    values = jax.random.normal(own_key, dims, jnp.float32) * scale * level
    return jnp.minimum(jnp.maximum(values, -most), most).astype(kind)


def setup_inputs(seed: int = 0, part: int = 0) -> dict:
    splits = jax.random.split(jax.random.key(seed), 8)
    own_keys = jax.random.split(jax.random.fold_in(splits[7], part), 8)
    return {
        "event_ids": place_ends(skewed_ids(own_keys[0], (TOKENS,), V, 2), jax.random.fold_in(own_keys[0], 3), 0, V - 1).astype(jnp.int32),
        "embed_table": normal_values(splits[1], (V, D), 1.0, 6.0),
        "w_qkv": normal_values(splits[2], (D, H * 3 * DH), D ** -0.5, 0.1875, ((1, 4),)),
        "norm_gain": jnp.clip(1.0 + 0.18 * jax.random.normal(splits[3], (H * DH,), jnp.float32), 0.1, 1.9),
        "w_out": normal_values(splits[4], (H * DH, D), (H * DH) ** -0.5, 0.1875, ((0, 4),)),
        "init_state": normal_values(splits[5], (H, DH, DH), 1.0, 6.0, ((0, 4),), jnp.float32),
        "out_grad": normal_values(own_keys[6], (TOKENS, D), (4.0 * TOKENS ** -0.5), 1.0, ((0, 4),)),
    }


EPS = 1e-05

def lower_mask():
    rows_idx = lax.broadcasted_iota(jnp.int32, (BLOCK, BLOCK), 0)
    cols_idx = lax.broadcasted_iota(jnp.int32, (BLOCK, BLOCK), 1)
    return rows_idx >= cols_idx

def reference(event_ids, embed_table, w_qkv, norm_gain, w_out, init_state, out_grad):
    highest = lax.Precision.HIGHEST
    tokens_all = event_ids.shape[0]
    blocks = tokens_all // BLOCK
    embedded = embed_table[event_ids]
    projected = jnp.dot(embedded, w_qkv, preferred_element_type=jnp.float32).astype(jnp.bfloat16)
    shaped = projected.reshape(blocks, BLOCK, H, 3, DH).astype(jnp.float32)
    queries = shaped[:, :, :, 0]
    key_rows = shaped[:, :, :, 1]
    value_rows = shaped[:, :, :, 2]
    block_kv = jnp.einsum('bshd,bshe->bhde', key_rows, value_rows, precision=highest)
    cumulative = jnp.cumsum(block_kv, axis=0)
    shifted = jnp.concatenate([jnp.zeros_like(block_kv[:1]), cumulative[:-1]], axis=0)
    states = init_state[None] + shifted
    mask_tri = lower_mask()[None, None]
    scores = jnp.einsum('bthd,bshd->bhts', queries, key_rows, precision=highest)
    scores_bf = jnp.where(mask_tri, scores, 0.0).astype(jnp.bfloat16).astype(jnp.float32)
    inter = jnp.einsum('bthd,bhde->bthe', queries, states, precision=highest)
    intra = jnp.einsum('bhts,bshe->bthe', scores_bf, value_rows, precision=highest)
    raw_out = inter + intra
    inv_rms = lax.rsqrt(lax.optimization_barrier(jnp.mean(raw_out * raw_out, axis=-1, keepdims=True)) + EPS)
    normed = raw_out * inv_rms
    gain_view = norm_gain.reshape(H, DH)
    attn = (normed * gain_view).astype(jnp.bfloat16).reshape(tokens_all, H * DH)
    layer_out = (embedded.astype(jnp.float32) + jnp.dot(attn, w_out, preferred_element_type=jnp.float32)).astype(jnp.bfloat16)
    grad_attn = jnp.dot(out_grad, w_out.T, preferred_element_type=jnp.float32)
    grad_wout = jnp.dot(attn.T, out_grad, preferred_element_type=jnp.float32)
    normed_flat = normed.reshape(tokens_all, H * DH)
    grad_gain = lax.optimization_barrier(jnp.sum(grad_attn * normed_flat, axis=0))
    grad_norm = (grad_attn * norm_gain).reshape(blocks, BLOCK, H, DH)
    grad_raw = inv_rms * (grad_norm - normed * lax.optimization_barrier(jnp.mean(grad_norm * normed, axis=-1, keepdims=True)))
    grad_bf = grad_raw.astype(jnp.bfloat16).astype(jnp.float32)
    grad_scores = jnp.einsum('bthe,bshe->bhts', grad_bf, value_rows, precision=highest)
    grad_scores = jnp.where(mask_tri, grad_scores, 0.0).astype(jnp.bfloat16).astype(jnp.float32)
    block_qg = jnp.einsum('bthd,bthe->bhde', queries, grad_bf, precision=highest)
    reversed_sum = jnp.cumsum(block_qg[::-1], axis=0)[::-1]
    after = jnp.concatenate([reversed_sum[1:], jnp.zeros_like(block_qg[:1])], axis=0)
    grad_q = jnp.einsum('bthe,bhde->bthd', grad_bf, states, precision=highest) + jnp.einsum('bhts,bshd->bthd', grad_scores, key_rows, precision=highest)
    grad_k = jnp.einsum('bshe,bhde->bshd', value_rows, after, precision=highest) + jnp.einsum('bhts,bthd->bshd', grad_scores, queries, precision=highest)
    grad_v = jnp.einsum('bshd,bhde->bshe', key_rows, after, precision=highest) + jnp.einsum('bhts,bthe->bshe', scores_bf, grad_bf, precision=highest)
    grad_proj = jnp.stack([grad_q, grad_k, grad_v], axis=3).astype(jnp.bfloat16).reshape(tokens_all, H * 3 * DH)
    grad_init = lax.optimization_barrier(jnp.sum(block_qg, axis=0))
    grad_wqkv = jnp.dot(embedded.T, grad_proj, preferred_element_type=jnp.float32)
    grad_embedded = out_grad.astype(jnp.float32) + jnp.dot(grad_proj, w_qkv.T, preferred_element_type=jnp.float32)
    hot_float = (event_ids[:, None] == jnp.arange(V, dtype=jnp.int32)[None, :]).astype(jnp.float32)
    grad_table = jnp.dot(hot_float.T, grad_embedded, precision=highest)
    return (layer_out, grad_wqkv, grad_wout, grad_gain, grad_init, grad_table)
```

```python
import functools
import jax
import jax.numpy as jnp
from jax import lax
from jax.experimental import pallas as pl
from jax.experimental.pallas import tpu as pltpu
from jax.sharding import PartitionSpec as P

BLOCK = 128


EPS = 1e-05


def prefix(part, axis, combine, identity, reverse):
    count = lax.axis_size(axis)
    place = lax.axis_index(axis)
    ahead = count - 1 - place if reverse else place
    gathered = lax.all_gather(part, axis)
    state = jnp.zeros_like(part) + jnp.asarray(identity, part.dtype)

    def one(step, state):
        source = count - 1 - step if reverse else step
        return combine(state, lax.dynamic_index_in_dim(gathered, source, 0, False))

    return lax.fori_loop(0, ahead, one, state)


def lower_mask(block_len):
    rows_idx = lax.broadcasted_iota(jnp.int32, (block_len, block_len), 0)
    cols_idx = lax.broadcasted_iota(jnp.int32, (block_len, block_len), 1)
    return rows_idx >= cols_idx


def add_states(earlier, later_one):
    return earlier + later_one


def contract_rows(left, right):
    return lax.dot_general(
        left, right, (((0,), (0,)), ((), ())), preferred_element_type=jnp.float32
    )


def contract_cols(left, right):
    return lax.dot_general(
        left, right, (((1,), (1,)), ((), ())), preferred_element_type=jnp.float32
    )


def per_device(event_ids, embed_table, w_qkv, norm_gain, w_out, init_state, out_grad):
    highest = lax.Precision.HIGHEST
    tok_rows = event_ids.shape[0]
    vocab_size = embed_table.shape[0]
    head_local = init_state.shape[0]
    head_dim = init_state.shape[1]
    block_len = BLOCK
    blocks = tok_rows // block_len
    one_hot = event_ids[:, None] == lax.broadcasted_iota(jnp.int32, (1, vocab_size), 1)
    embedded = jnp.dot(
        one_hot.astype(jnp.bfloat16), embed_table, preferred_element_type=jnp.float32
    ).astype(jnp.bfloat16)
    projected = jnp.dot(embedded, w_qkv, preferred_element_type=jnp.float32).astype(jnp.bfloat16)
    shaped = projected.reshape(blocks, block_len, head_local, 3, head_dim)
    queries = shaped[:, :, :, 0]
    key_rows = shaped[:, :, :, 1]
    value_rows = shaped[:, :, :, 2]
    block_kv = jnp.einsum(
        "bshd,bshe->bhde", key_rows, value_rows, preferred_element_type=jnp.float32
    )
    own_total = jnp.sum(block_kv, axis=0)
    zero_state = jnp.zeros_like(own_total)
    earlier_state = prefix(own_total, "ctx", add_states, zero_state, False)
    cumulative = jnp.cumsum(block_kv, axis=0)
    shifted = jnp.concatenate([jnp.zeros_like(block_kv[:1]), cumulative[:-1]], axis=0)
    states = init_state[None] + earlier_state[None] + shifted
    mask_tri = lower_mask(block_len)[None, None]
    scores = jnp.einsum("bthd,bshd->bhts", queries, key_rows, preferred_element_type=jnp.float32)
    scores_bf = jnp.where(mask_tri, scores, 0.0).astype(jnp.bfloat16)
    inter = jnp.einsum("bthd,bhde->bthe", queries.astype(jnp.float32), states, precision=highest)
    intra = jnp.einsum("bhts,bshe->bthe", scores_bf, value_rows, preferred_element_type=jnp.float32)
    raw_out = inter + intra
    inv_rms = lax.rsqrt(jnp.mean(raw_out * raw_out, axis=-1, keepdims=True) + EPS)
    normed = raw_out * inv_rms
    gain_view = norm_gain.reshape(head_local, head_dim)
    attn = (normed * gain_view).astype(jnp.bfloat16).reshape(tok_rows, head_local * head_dim)
    head_terms = jnp.dot(attn, w_out, preferred_element_type=jnp.float32)
    mixed = lax.psum_scatter(head_terms, "head", scatter_dimension=1, tiled=True)
    out_cols = mixed.shape[1]
    residual = lax.dynamic_slice_in_dim(embedded, lax.axis_index("head") * out_cols, out_cols, 1)
    layer_out = (residual.astype(jnp.float32) + mixed).astype(jnp.bfloat16)
    grad_attn = contract_cols(out_grad, w_out)
    grad_wout_local = contract_rows(attn, out_grad)
    normed_flat = normed.reshape(tok_rows, head_local * head_dim)
    grad_gain_local = jnp.sum(grad_attn * normed_flat, axis=0)
    grad_norm = (grad_attn * norm_gain).reshape(blocks, block_len, head_local, head_dim)
    grad_raw = inv_rms * (grad_norm - normed * jnp.mean(grad_norm * normed, axis=-1, keepdims=True))
    grad_bf = grad_raw.astype(jnp.bfloat16)
    grad_scores = jnp.einsum(
        "bthe,bshe->bhts", grad_bf, value_rows, preferred_element_type=jnp.float32
    )
    grad_scores = jnp.where(mask_tri, grad_scores, 0.0).astype(jnp.bfloat16)
    block_qg = jnp.einsum("bthd,bthe->bhde", queries, grad_bf, preferred_element_type=jnp.float32)
    own_grad = jnp.sum(block_qg, axis=0)
    later_state = prefix(own_grad, "ctx", add_states, zero_state, True)
    reversed_sum = jnp.cumsum(block_qg[::-1], axis=0)[::-1]
    local_after = jnp.concatenate([reversed_sum[1:], jnp.zeros_like(block_qg[:1])], axis=0)
    after = later_state[None] + local_after
    grad_q = jnp.einsum(
        "bthe,bhde->bthd", grad_bf.astype(jnp.float32), states, precision=highest
    ) + jnp.einsum("bhts,bshd->bthd", grad_scores, key_rows, preferred_element_type=jnp.float32)
    grad_k = jnp.einsum(
        "bshe,bhde->bshd", value_rows.astype(jnp.float32), after, precision=highest
    ) + jnp.einsum("bhts,bthd->bshd", grad_scores, queries, preferred_element_type=jnp.float32)
    grad_v = jnp.einsum(
        "bshd,bhde->bshe", key_rows.astype(jnp.float32), after, precision=highest
    ) + jnp.einsum("bhts,bthe->bshe", scores_bf, grad_bf, preferred_element_type=jnp.float32)
    grad_proj = (
        jnp.stack([grad_q, grad_k, grad_v], axis=3)
        .astype(jnp.bfloat16)
        .reshape(tok_rows, head_local * 3 * head_dim)
    )
    vocab_proj = contract_rows(one_hot.astype(jnp.bfloat16), grad_proj)
    vocab_cot = contract_rows(one_hot.astype(jnp.bfloat16), out_grad)
    summed_vocab, summed_wout, summed_gain, grad_init, summed_cot = lax.psum(
        (vocab_proj, grad_wout_local, grad_gain_local, own_grad, vocab_cot), "ctx"
    )
    summed_wqkv = lax.dot_general(
        embed_table.astype(jnp.float32),
        summed_vocab,
        (((0,), (0,)), ((), ())),
        precision=highest,
        preferred_element_type=jnp.float32,
    )
    head_table = lax.dot_general(
        summed_vocab,
        w_qkv.astype(jnp.float32),
        (((1,), (1,)), ((), ())),
        precision=highest,
        preferred_element_type=jnp.float32,
    )
    grad_table = lax.psum(head_table, "head") + summed_cot
    ctx_pos = lax.axis_index("ctx")
    width_rows = summed_wqkv.shape[0] // lax.axis_size("ctx")
    own_wqkv = lax.dynamic_slice_in_dim(summed_wqkv, ctx_pos * width_rows, width_rows, 0)
    own_wout = lax.dynamic_slice_in_dim(summed_wout, ctx_pos * width_rows, width_rows, 1)
    return (layer_out, own_wqkv, own_wout, summed_gain, grad_init, grad_table)


F32 = jnp.float32
BF16 = jnp.bfloat16
CHUNKS = 4


def nn(left, right):
    return lax.dot_general(left, right, (((1,), (0,)), ((), ())), preferred_element_type=F32)


def split(value):
    high = value.astype(BF16)
    return high, (value - high.astype(F32)).astype(BF16)


def layer_kernel(
    dims,
    ids, table, wqkv, gain, wout, init, cot,
    layer_out, grad_wqkv, grad_wout, grad_gain, grad_init, grad_table,
    hot, tables, proj, gproj, scores, kv_loc, qg_loc, gattn, local_kv, grad_bf, attn_bf,
    kv_own, kv_recv, kv_stage, qg_own, qg_recv, qg_stage,
    wo_send, wo_recv, attn_send, attn_recv, gw_own, gw_recv,
    voc_own, voc_recv, voc_stage, head_part, core_recv, pair_sum, cross_recv,
    kv_ss, kv_rs, qg_ss, qg_rs, wo_ss, wo_rs, at_ss, at_rs, gw_ss, gw_rs,
    voc_ss, voc_rs, tab_ss, tab_rs,
):
    C, tok, vocab, width, heads, dh = dims
    blocks = tok // BLOCK
    cols = heads * dh
    three = 3 * cols
    part = lax.axis_index("parts")
    c = lax.axis_index("ctx")
    h = lax.axis_index("head")
    core = lax.rem(h, 2)
    sib = h + 1 - 2 * core
    across = lax.rem(h + 2, 4)
    diag = lax.rem(sib + 2, 4)
    peers = (sib, across, diag)
    far_end = C - 1
    near = c // (C // 2)
    own_cols = pl.ds(pl.multiple_of(h * cols, cols), cols)

    def remote(src, dst, ss, rs, ctx_to, head_to):
        return pltpu.make_async_remote_copy(
            src_ref=src, dst_ref=dst, send_sem=ss, recv_sem=rs,
            device_id=(part, ctx_to, head_to), device_id_type=pl.DeviceIdType.MESH,
        )

    barrier = pltpu.get_barrier_semaphore()
    for step in range(1, C):
        pl.semaphore_signal(barrier, inc=1, device_id=(part, lax.rem(c + step, C), h),
                            device_id_type=pl.DeviceIdType.MESH)
    for peer in peers:
        pl.semaphore_signal(barrier, inc=1, device_id=(part, c, peer),
                            device_id_type=pl.DeviceIdType.MESH)

    def has_recv(d):
        return jnp.where(d == 0, c > 0, c < far_end)

    def has_send(d):
        return jnp.where(d == 0, c < far_end, c > 0)

    def line_copy(d, i, recv, stage, ss, rs):
        to = jnp.clip(c + 1 - 2 * d, 0, far_end)
        return remote(stage.at[d, i], recv.at[d, i], ss.at[d, i], rs.at[d, i], to, h)

    def line(d, i, own, recv, stage, ss, rs):
        @pl.when(has_recv(d))
        def _():
            line_copy(d, i, recv, stage, ss, rs).wait_recv()

        @pl.when(jnp.logical_not(has_recv(d)))
        def _():
            recv[d, i] = jnp.zeros(recv.shape[2:], F32)

        @pl.when(has_send(d))
        def _():
            stage[d, i] = own[i] + recv[d, i]
            line_copy(d, i, recv, stage, ss, rs).start()

    def line_sent(d, i, recv, stage, ss, rs):
        @pl.when(has_send(d))
        def _():
            line_copy(d, i, recv, stage, ss, rs).wait_send()

    kv = (kv_own, kv_recv, kv_stage, kv_ss, kv_rs)
    qg = (qg_own, qg_recv, qg_stage, qg_ss, qg_rs)
    voc = (voc_own, voc_recv, voc_stage, voc_ss, voc_rs)

    hot[...] = (lax.broadcasted_iota(jnp.int32, (vocab, tok), 0) == ids[...]).astype(BF16)
    tables[:, :three] = nn(table[...], wqkv[...]).astype(BF16)
    tables[:, three:] = table[:, own_cols]

    def project(i, carry):
        at = pl.ds(pl.multiple_of(i * 256, 256), 256)
        proj[at, :] = contract_rows(hot[:, at], tables[...]).astype(BF16)
        return carry

    lax.fori_loop(0, tok // 256, project, 0)

    kv_own[...] = jnp.zeros_like(kv_own)

    def qkv(b, head):
        at = pl.ds(pl.multiple_of(b * BLOCK, BLOCK), BLOCK)
        base = head * 3 * dh
        return (proj[at, base:base + dh], proj[at, base + dh:base + 2 * dh],
                proj[at, base + 2 * dh:base + 3 * dh])

    def key_values(b, carry):
        for head in range(heads):
            _, k, v = qkv(b, head)
            kv_loc[b, head] = kv_own[head]
            kv_own[head] = kv_own[head] + contract_rows(k, v)
        return carry

    lax.fori_loop(0, blocks, key_values, 0)

    pl.semaphore_wait(barrier, C - 1 + len(peers))

    def kv_step(place):
        @pl.when(c == place)
        def _():
            for head in range(heads):
                line(0, head, *kv)

    kv_step(0)

    def wo_copy(n):
        return remote(wo_send.at[peers[n]], wo_recv.at[h], wo_ss.at[n], wo_rs.at[n], c, peers[n])

    for block in range(4):
        wo_send[block] = wout[:, block * cols:(block + 1) * cols].astype(F32)
    for n in range(3):
        wo_copy(n).start()

    def cotangent(i, carry):
        at = pl.ds(pl.multiple_of(i * 256, 256), 256)
        gattn[at, :] = contract_cols(cot[at, :], wout[...])
        return carry

    lax.fori_loop(0, tok // 256, cotangent, 0)
    kv_step(1)

    mask = lower_mask(BLOCK)

    def score(b, carry):
        for head in range(heads):
            q, k, _ = qkv(b, head)
            scores[b, head] = jnp.where(mask, contract_cols(q, k), 0.0).astype(BF16)
        return carry

    lax.fori_loop(0, blocks, score, 0)
    kv_step(2)

    per = vocab // CHUNKS
    for i in range(CHUNKS):
        voc_own[i, :, three:] = nn(hot[i * per:(i + 1) * per, :], cot[:, own_cols])
    for place in range(3, C):
        kv_step(place)

    qg_own[...] = jnp.zeros_like(qg_own)
    for head in range(heads):
        kv_own[head] = init[head] + kv_recv[0, head]

    def forward(b, carry):
        at = pl.ds(pl.multiple_of(b * BLOCK, BLOCK), BLOCK)
        for head in range(heads):
            q, k, v = qkv(b, head)
            mine = slice(head * dh, (head + 1) * dh)
            state = kv_loc[b, head] + kv_own[head]
            kv_loc[b, head] = state
            high, low = split(state)
            raw = nn(q, high) + nn(q, low) + nn(scores[b, head], v)
            inv = lax.rsqrt(jnp.mean(raw * raw, axis=-1, keepdims=True) + EPS)
            normed = raw * inv
            g_row = gain[head:head + 1, :]
            attn = (normed * g_row).astype(BF16)
            attn_bf[at, mine] = attn
            attn_send[at, mine] = attn.astype(F32)
            ga = gattn[at, mine]
            qg_own[heads, head:head + 1, :] += jnp.sum(ga * normed, axis=0, keepdims=True)
            dn = ga * g_row
            g = inv * (dn - normed * jnp.mean(dn * normed, axis=-1, keepdims=True))
            g = g.astype(BF16)
            grad_bf[at, mine] = g
            outer = contract_rows(q, g)
            qg_loc[b, head] = outer
            qg_own[head] += outer
        return carry

    lax.fori_loop(0, blocks, forward, 0)

    at_sib = remote(attn_send, attn_recv.at[h], at_ss.at[0], at_rs.at[0], c, sib)
    at_across = remote(attn_send, attn_recv.at[h], at_ss.at[1], at_rs.at[1], c, across)
    at_relay = remote(attn_recv.at[across], attn_recv.at[across], at_ss.at[2], at_rs.at[2], c, sib)

    at_end = jnp.logical_or(c == 0, c == far_end)

    def qg_step(where, d):
        @pl.when(where)
        def _():
            for piece in range(heads + 1):
                line(d, piece, *qg)

    qg_step(at_end, near)
    at_sib.start()
    at_across.start()

    def weight(i, carry):
        gw_own[i] = contract_rows(
            attn_bf[...], cot[:, pl.ds(pl.multiple_of(i * cols, cols), cols)])
        return carry

    lax.fori_loop(0, C, weight, 0)
    qg_step(jnp.logical_not(at_end), near)

    def backward(b, carry):
        at = pl.ds(pl.multiple_of(b * BLOCK, BLOCK), BLOCK)
        for head in range(heads):
            q, k, v = qkv(b, head)
            base = head * 3 * dh
            g = grad_bf[at, head * dh:(head + 1) * dh]
            high, low = split(kv_loc[b, head])
            gs = jnp.where(mask, contract_cols(g, v), 0.0).astype(BF16)
            dq = contract_cols(g, high) + contract_cols(g, low) + nn(gs, k)
            gproj[at, base:base + dh] = dq.astype(BF16)
            local_kv[at, head * 2 * dh:head * 2 * dh + dh] = contract_rows(gs, q)
            local_kv[at, head * 2 * dh + dh:(head + 1) * 2 * dh] = contract_rows(scores[b, head], g)
        return carry

    half = blocks // 2
    lax.fori_loop(0, half, backward, 0)
    qg_step(jnp.logical_not(at_end), 1 - near)
    lax.fori_loop(half, blocks, backward, 0)
    qg_step(at_end, 1 - near)

    def gw_copy(step):
        to = lax.rem(c + step, C)
        return remote(gw_own.at[to], gw_recv.at[step - 1], gw_ss.at[step - 1],
                      gw_rs.at[step - 1], to, h)

    for step in range(1, C):
        gw_copy(step).start()

    for head in range(heads):
        grad_init[head] = qg_own[head] + (qg_recv[0, head] + qg_recv[1, head])
    grad_gain[...] = (qg_own[heads] + (qg_recv[0, heads] + qg_recv[1, heads]))[:heads, :]
    for head in range(heads):
        kv_own[head] = qg_recv[1, head]

    def later(step, carry):
        b = blocks - 1 - step
        at = pl.ds(pl.multiple_of(b * BLOCK, BLOCK), BLOCK)
        for head in range(heads):
            _, k, v = qkv(b, head)
            base = head * 3 * dh
            after = kv_own[head]
            high, low = split(after)
            kv_own[head] = after + qg_loc[b, head]
            dk = local_kv[at, head * 2 * dh:head * 2 * dh + dh]
            dv = local_kv[at, head * 2 * dh + dh:(head + 1) * 2 * dh]
            dk = dk + contract_cols(v, high) + contract_cols(v, low)
            dv = dv + nn(k, high) + nn(k, low)
            gproj[at, base + dh:base + 2 * dh] = dk.astype(BF16)
            gproj[at, base + 2 * dh:base + 3 * dh] = dv.astype(BF16)
        return carry

    lax.fori_loop(0, blocks, later, 0)

    for i in range(CHUNKS):
        voc_own[i, :, :three] = nn(hot[i * per:(i + 1) * per, :], gproj[...])

        @pl.when(at_end)
        def _():
            line(near, i, *voc)

    at_across.wait_recv()
    at_relay.start()

    half_rows = per // 2
    my_half = pl.ds(pl.multiple_of(core * half_rows, half_rows), half_rows)
    sib_half = pl.ds(pl.multiple_of((1 - core) * half_rows, half_rows), half_rows)

    def core_copy(i):
        return remote(head_part.at[i, sib_half, :], core_recv.at[i],
                      tab_ss.at[0, i], tab_rs.at[0, i], c, sib)

    def cross_copy(i):
        return remote(pair_sum.at[i], cross_recv.at[i], tab_ss.at[1, i], tab_rs.at[1, i], c, across)

    def final_copy(i):
        rows = pl.ds(pl.multiple_of(i * per + core * half_rows, half_rows), half_rows)
        return remote(grad_table.at[rows, :], grad_table.at[rows, :],
                      tab_ss.at[2, i], tab_rs.at[2, i], c, sib)

    def start_head(i):
        total = voc_own[i] + (voc_recv[0, i] + voc_recv[1, i])
        voc_own[i] = total
        high, low = split(total[:, :three])
        head_part[i] = contract_cols(high, wqkv[...]) + contract_cols(low, wqkv[...])
        head_part[i, :, own_cols] = head_part[i, :, own_cols] + total[:, three:]
        core_copy(i).start()

    def start_cross(i):
        core_copy(i).wait_recv()
        pair_sum[i] = head_part[i, my_half, :] + core_recv[i]
        cross_copy(i).start()

    def start_final(i):
        cross_copy(i).wait_recv()
        rows = pl.ds(pl.multiple_of(i * per + core * half_rows, half_rows), half_rows)
        grad_table[rows, :] = pair_sum[i] + cross_recv[i]
        final_copy(i).start()

    for i in range(CHUNKS + 1):
        if i < CHUNKS:
            @pl.when(jnp.logical_not(at_end))
            def _():
                line(near, i, *voc)
        if i > 0:
            @pl.when(jnp.logical_not(at_end))
            def _():
                line(1 - near, i - 1, *voc)

            @pl.when(at_end)
            def _():
                line(1 - near, i - 1, *voc)

            start_head(i - 1)
            if i > 1:
                start_cross(i - 2)
            if i > 2:
                start_final(i - 3)

    start_cross(CHUNKS - 1)

    at_sib.wait_recv()
    at_relay.wait_recv()
    for n in range(3):
        remote(wo_send.at[peers[n]], wo_recv.at[peers[n]], wo_ss.at[n], wo_rs.at[n], c, peers[n]).wait_recv()
    wo_recv[h] = wout[:, own_cols].astype(F32)

    def out_rows(i, carry):
        at = pl.ds(pl.multiple_of(i * 256, 256), 256)
        mixed = nn(attn_bf[at, :], wo_recv[h].astype(BF16))
        for peer in peers:
            mixed = mixed + nn(attn_recv[peer, at, :].astype(BF16), wo_recv[peer].astype(BF16))
        layer_out[at, :] = (proj[at, three:].astype(F32) + mixed).astype(BF16)
        return carry

    lax.fori_loop(0, tok // 256, out_rows, 0)
    start_final(CHUNKS - 2)

    rows = pl.ds(pl.multiple_of(c * (width // C), width // C), width // C)
    total_w = jnp.zeros((width // C, three), F32)
    for i in range(CHUNKS):
        high, low = split(voc_own[i, :, :three])
        mine = table[i * per:(i + 1) * per, rows]
        total_w = total_w + contract_rows(mine, high) + contract_rows(mine, low)
    grad_wqkv[...] = total_w
    start_final(CHUNKS - 1)

    for step in range(1, C):
        gw_copy(step).wait_recv()
    grad_wout[...] = (gw_own[c] + gw_recv[0]) + (gw_recv[1] + gw_recv[2])

    for i in range(CHUNKS):
        other = pl.ds(pl.multiple_of(i * per + (1 - core) * half_rows, half_rows), half_rows)
        remote(grad_table.at[other, :], grad_table.at[other, :],
               tab_ss.at[2, i], tab_rs.at[2, i], c, sib).wait_recv()
        core_copy(i).wait_send()
        cross_copy(i).wait_send()
        final_copy(i).wait_send()
        for d in range(2):
            line_sent(d, i, *voc[1:])
    for head in range(heads):
        line_sent(0, head, *kv[1:])
    for piece in range(heads + 1):
        for d in range(2):
            line_sent(d, piece, *qg[1:])
    for n in range(3):
        wo_copy(n).wait_send()
    for step in range(1, C):
        gw_copy(step).wait_send()
    at_sib.wait_send()
    at_across.wait_send()
    at_relay.wait_send()


def one_kernel(event_ids, embed_table, w_qkv, norm_gain, w_out, init_state, out_grad):
    tok, = event_ids.shape
    vocab, width = embed_table.shape
    heads, dh, _ = init_state.shape
    C = lax.axis_size("ctx")
    cols = heads * dh
    three = 3 * cols
    blocks = tok // BLOCK
    per = vocab // CHUNKS
    vmem = lambda *shape: pltpu.VMEM(shape, F32)
    half = lambda *shape: pltpu.VMEM(shape, BF16)
    dma = lambda *shape: pltpu.SemaphoreType.DMA(shape)
    shapes = [
        half(vocab, tok), half(vocab, three + cols), half(tok, three + cols), half(tok, three),
        half(blocks, heads, BLOCK, BLOCK), vmem(blocks, heads, dh, dh), vmem(blocks, heads, dh, dh),
        vmem(tok, cols), vmem(tok, 2 * cols), half(tok, cols), half(tok, cols),
        vmem(heads, dh, dh), vmem(1, heads, dh, dh), vmem(1, heads, dh, dh),
        vmem(heads + 1, dh, dh), vmem(2, heads + 1, dh, dh), vmem(2, heads + 1, dh, dh),
        vmem(4, cols, cols), vmem(4, cols, cols), vmem(tok, cols), vmem(4, tok, cols),
        vmem(C, cols, width // C), vmem(C - 1, cols, width // C),
        vmem(CHUNKS, per, width), vmem(2, CHUNKS, per, width), vmem(2, CHUNKS, per, width),
        vmem(CHUNKS, per, width), vmem(CHUNKS, per // 2, width), vmem(CHUNKS, per // 2, width),
        vmem(CHUNKS, per // 2, width),
        dma(1, heads), dma(1, heads), dma(2, heads + 1), dma(2, heads + 1), dma(3), dma(3),
        dma(3), dma(3), dma(C - 1), dma(C - 1), dma(2, CHUNKS), dma(2, CHUNKS),
        dma(3, CHUNKS), dma(3, CHUNKS),
    ]
    outs = pl.pallas_call(
        functools.partial(layer_kernel, (C, tok, vocab, width, heads, dh)),
        out_shape=(
            jax.ShapeDtypeStruct((tok, cols), BF16),
            jax.ShapeDtypeStruct((width // C, three), F32),
            jax.ShapeDtypeStruct((cols, width // C), F32),
            jax.ShapeDtypeStruct((heads, dh), F32),
            jax.ShapeDtypeStruct((heads, dh, dh), F32),
            jax.ShapeDtypeStruct((vocab, width), F32),
        ),
        in_specs=[pl.BlockSpec(memory_space=pltpu.VMEM)] * 7,
        out_specs=(pl.BlockSpec(memory_space=pltpu.VMEM),) * 6,
        scratch_shapes=shapes,
        compiler_params=pltpu.CompilerParams(
            collective_id=0, has_side_effects=True, vmem_limit_bytes=56 * 1024 * 1024
        ),
    )(event_ids.reshape(1, tok), embed_table, w_qkv, norm_gain.reshape(heads, dh), w_out,
      init_state, out_grad)
    layer_out, grad_wqkv, grad_wout, grad_gain, grad_init, grad_table = outs
    return layer_out, grad_wqkv, grad_wout, grad_gain.reshape(cols), grad_init, grad_table


def solution(mesh):
    in_specs = (
        P(("parts", "ctx")),
        P(),
        P(None, "head"),
        P("head"),
        P("head", None),
        P("head", None, None),
        P(("parts", "ctx"), None),
    )
    out_specs = (
        P(("parts", "ctx"), "head"),
        P(("parts", "ctx"), "head"),
        P(("parts", "head"), "ctx"),
        P(("parts", "head")),
        P(("parts", "head"), None, None),
        P("parts", None),
    )
    fits = mesh.shape["ctx"] == 4 and mesh.shape["head"] == 4
    return jax.shard_map(
        one_kernel if fits else per_device, mesh=mesh, in_specs=in_specs, out_specs=out_specs, check_vma=False
    )
```

```python
import functools
import jax
import jax.numpy as jnp
from jax import lax
from jax.experimental import pallas as pl
from jax.experimental.pallas import tpu as pltpu
from jax.sharding import PartitionSpec as P

BLOCK = 128


EPS = 1e-05


def prefix(part, axis, combine, identity, reverse):
    count = lax.axis_size(axis)
    place = lax.axis_index(axis)
    ahead = count - 1 - place if reverse else place
    gathered = lax.all_gather(part, axis)
    state = jnp.zeros_like(part) + jnp.asarray(identity, part.dtype)

    def one(step, state):
        source = count - 1 - step if reverse else step
        return combine(state, lax.dynamic_index_in_dim(gathered, source, 0, False))

    return lax.fori_loop(0, ahead, one, state)


def lower_mask(block_len):
    rows_idx = lax.broadcasted_iota(jnp.int32, (block_len, block_len), 0)
    cols_idx = lax.broadcasted_iota(jnp.int32, (block_len, block_len), 1)
    return rows_idx >= cols_idx


def add_states(earlier, later_one):
    return earlier + later_one


def contract_rows(left, right):
    return lax.dot_general(
        left, right, (((0,), (0,)), ((), ())), preferred_element_type=jnp.float32
    )


def contract_cols(left, right):
    return lax.dot_general(
        left, right, (((1,), (1,)), ((), ())), preferred_element_type=jnp.float32
    )


def per_device(event_ids, embed_table, w_qkv, norm_gain, w_out, init_state, out_grad):
    highest = lax.Precision.HIGHEST
    tok_rows = event_ids.shape[0]
    vocab_size = embed_table.shape[0]
    head_local = init_state.shape[0]
    head_dim = init_state.shape[1]
    block_len = BLOCK
    blocks = tok_rows // block_len
    one_hot = event_ids[:, None] == lax.broadcasted_iota(jnp.int32, (1, vocab_size), 1)
    embedded = jnp.dot(
        one_hot.astype(jnp.bfloat16), embed_table, preferred_element_type=jnp.float32
    ).astype(jnp.bfloat16)
    projected = jnp.dot(embedded, w_qkv, preferred_element_type=jnp.float32).astype(jnp.bfloat16)
    shaped = projected.reshape(blocks, block_len, head_local, 3, head_dim)
    queries = shaped[:, :, :, 0]
    key_rows = shaped[:, :, :, 1]
    value_rows = shaped[:, :, :, 2]
    block_kv = jnp.einsum(
        "bshd,bshe->bhde", key_rows, value_rows, preferred_element_type=jnp.float32
    )
    own_total = jnp.sum(block_kv, axis=0)
    zero_state = jnp.zeros_like(own_total)
    earlier_state = prefix(own_total, "ctx", add_states, zero_state, False)
    cumulative = jnp.cumsum(block_kv, axis=0)
    shifted = jnp.concatenate([jnp.zeros_like(block_kv[:1]), cumulative[:-1]], axis=0)
    states = init_state[None] + earlier_state[None] + shifted
    mask_tri = lower_mask(block_len)[None, None]
    scores = jnp.einsum("bthd,bshd->bhts", queries, key_rows, preferred_element_type=jnp.float32)
    scores_bf = jnp.where(mask_tri, scores, 0.0).astype(jnp.bfloat16)
    inter = jnp.einsum("bthd,bhde->bthe", queries.astype(jnp.float32), states, precision=highest)
    intra = jnp.einsum("bhts,bshe->bthe", scores_bf, value_rows, preferred_element_type=jnp.float32)
    raw_out = inter + intra
    inv_rms = lax.rsqrt(jnp.mean(raw_out * raw_out, axis=-1, keepdims=True) + EPS)
    normed = raw_out * inv_rms
    gain_view = norm_gain.reshape(head_local, head_dim)
    attn = (normed * gain_view).astype(jnp.bfloat16).reshape(tok_rows, head_local * head_dim)
    head_terms = jnp.dot(attn, w_out, preferred_element_type=jnp.float32)
    mixed = lax.psum_scatter(head_terms, "head", scatter_dimension=1, tiled=True)
    out_cols = mixed.shape[1]
    residual = lax.dynamic_slice_in_dim(embedded, lax.axis_index("head") * out_cols, out_cols, 1)
    layer_out = (residual.astype(jnp.float32) + mixed).astype(jnp.bfloat16)
    grad_attn = contract_cols(out_grad, w_out)
    grad_wout_local = contract_rows(attn, out_grad)
    normed_flat = normed.reshape(tok_rows, head_local * head_dim)
    grad_gain_local = jnp.sum(grad_attn * normed_flat, axis=0)
    grad_norm = (grad_attn * norm_gain).reshape(blocks, block_len, head_local, head_dim)
    grad_raw = inv_rms * (grad_norm - normed * jnp.mean(grad_norm * normed, axis=-1, keepdims=True))
    grad_bf = grad_raw.astype(jnp.bfloat16)
    grad_scores = jnp.einsum(
        "bthe,bshe->bhts", grad_bf, value_rows, preferred_element_type=jnp.float32
    )
    grad_scores = jnp.where(mask_tri, grad_scores, 0.0).astype(jnp.bfloat16)
    block_qg = jnp.einsum("bthd,bthe->bhde", queries, grad_bf, preferred_element_type=jnp.float32)
    own_grad = jnp.sum(block_qg, axis=0)
    later_state = prefix(own_grad, "ctx", add_states, zero_state, True)
    reversed_sum = jnp.cumsum(block_qg[::-1], axis=0)[::-1]
    local_after = jnp.concatenate([reversed_sum[1:], jnp.zeros_like(block_qg[:1])], axis=0)
    after = later_state[None] + local_after
    grad_q = jnp.einsum(
        "bthe,bhde->bthd", grad_bf.astype(jnp.float32), states, precision=highest
    ) + jnp.einsum("bhts,bshd->bthd", grad_scores, key_rows, preferred_element_type=jnp.float32)
    grad_k = jnp.einsum(
        "bshe,bhde->bshd", value_rows.astype(jnp.float32), after, precision=highest
    ) + jnp.einsum("bhts,bthd->bshd", grad_scores, queries, preferred_element_type=jnp.float32)
    grad_v = jnp.einsum(
        "bshd,bhde->bshe", key_rows.astype(jnp.float32), after, precision=highest
    ) + jnp.einsum("bhts,bthe->bshe", scores_bf, grad_bf, preferred_element_type=jnp.float32)
    grad_proj = (
        jnp.stack([grad_q, grad_k, grad_v], axis=3)
        .astype(jnp.bfloat16)
        .reshape(tok_rows, head_local * 3 * head_dim)
    )
    vocab_proj = contract_rows(one_hot.astype(jnp.bfloat16), grad_proj)
    vocab_cot = contract_rows(one_hot.astype(jnp.bfloat16), out_grad)
    summed_vocab, summed_wout, summed_gain, grad_init, summed_cot = lax.psum(
        (vocab_proj, grad_wout_local, grad_gain_local, own_grad, vocab_cot), "ctx"
    )
    summed_wqkv = lax.dot_general(
        embed_table.astype(jnp.float32),
        summed_vocab,
        (((0,), (0,)), ((), ())),
        precision=highest,
        preferred_element_type=jnp.float32,
    )
    head_table = lax.dot_general(
        summed_vocab,
        w_qkv.astype(jnp.float32),
        (((1,), (1,)), ((), ())),
        precision=highest,
        preferred_element_type=jnp.float32,
    )
    grad_table = lax.psum(head_table, "head") + summed_cot
    ctx_pos = lax.axis_index("ctx")
    width_rows = summed_wqkv.shape[0] // lax.axis_size("ctx")
    own_wqkv = lax.dynamic_slice_in_dim(summed_wqkv, ctx_pos * width_rows, width_rows, 0)
    own_wout = lax.dynamic_slice_in_dim(summed_wout, ctx_pos * width_rows, width_rows, 1)
    return (layer_out, own_wqkv, own_wout, summed_gain, grad_init, grad_table)


F32 = jnp.float32
BF16 = jnp.bfloat16
CHUNKS = 8


def nn(left, right):
    return lax.dot_general(left, right, (((1,), (0,)), ((), ())), preferred_element_type=F32)


def split(value):
    high = value.astype(BF16)
    return high, (value - high.astype(F32)).astype(BF16)


def layer_kernel(
    dims,
    ids, table, wqkv, gain, wout, init, cot,
    layer_out, grad_wqkv, grad_wout, grad_gain, grad_init, grad_table,
    hot, tables, proj, gproj, scores, kv_loc, qg_loc, gattn, local_kv, grad_bf, attn_bf,
    kv_own, kv_recv, kv_stage, qg_own, qg_recv, qg_stage, gn_own, gn_recv, gn_stage, ct_own, ct_recv, ct_stage,
    wo_send, wo_recv, attn_send, attn_recv, gw_own, gw_recv,
    voc_own, voc_recv, voc_stage, head_part, core_recv, pair_sum, cross_recv,
    kv_ss, kv_rs, qg_ss, qg_rs, gn_ss, gn_rs, ct_ss, ct_rs, wo_ss, wo_rs, at_ss, at_rs, gw_ss, gw_rs,
    voc_ss, voc_rs, tab_ss, tab_rs,
):
    C, tok, vocab, width, heads, dh = dims
    blocks = tok // BLOCK
    cols = heads * dh
    three = 3 * cols
    part = lax.axis_index("parts")
    c = lax.axis_index("ctx")
    h = lax.axis_index("head")
    core = lax.rem(h, 2)
    sib = h + 1 - 2 * core
    across = lax.rem(h + 2, 4)
    diag = lax.rem(sib + 2, 4)
    peers = (sib, across, diag)
    far_end = C - 1
    near = c // (C // 2)
    own_cols = pl.ds(pl.multiple_of(h * cols, cols), cols)

    def remote(src, dst, ss, rs, ctx_to, head_to):
        return pltpu.make_async_remote_copy(
            src_ref=src, dst_ref=dst, send_sem=ss, recv_sem=rs,
            device_id=(part, ctx_to, head_to), device_id_type=pl.DeviceIdType.MESH,
        )

    barrier = pltpu.get_barrier_semaphore()
    for step in range(1, C):
        pl.semaphore_signal(barrier, inc=1, device_id=(part, lax.rem(c + step, C), h),
                            device_id_type=pl.DeviceIdType.MESH)
    for peer in peers:
        pl.semaphore_signal(barrier, inc=1, device_id=(part, c, peer),
                            device_id_type=pl.DeviceIdType.MESH)

    def has_recv(d):
        return jnp.where(d == 0, c > 0, c < far_end)

    def has_send(d):
        return jnp.where(d == 0, c < far_end, c > 0)

    def line_copy(d, i, recv, stage, ss, rs):
        to = jnp.clip(c + 1 - 2 * d, 0, far_end)
        return remote(stage.at[d, i], recv.at[d, i], ss.at[d, i], rs.at[d, i], to, h)

    def line(d, i, own, recv, stage, ss, rs):
        @pl.when(has_recv(d))
        def _():
            line_copy(d, i, recv, stage, ss, rs).wait_recv()

        @pl.when(jnp.logical_not(has_recv(d)))
        def _():
            recv[d, i] = jnp.zeros(recv.shape[2:], F32)

        @pl.when(has_send(d))
        def _():
            stage[d, i] = own[i] + recv[d, i]
            line_copy(d, i, recv, stage, ss, rs).start()

    def line_sent(d, i, recv, stage, ss, rs):
        @pl.when(has_send(d))
        def _():
            line_copy(d, i, recv, stage, ss, rs).wait_send()

    kv = (kv_own, kv_recv, kv_stage, kv_ss, kv_rs)
    qg = (qg_own, qg_recv, qg_stage, qg_ss, qg_rs)
    gn = (gn_own, gn_recv, gn_stage, gn_ss, gn_rs)
    ct = (ct_own, ct_recv, ct_stage, ct_ss, ct_rs)
    voc = (voc_own, voc_recv, voc_stage, voc_ss, voc_rs)

    hot[...] = (lax.broadcasted_iota(jnp.int32, (vocab, tok), 0) == ids[...]).astype(BF16)
    quarter = vocab // 4
    for i in range(4):
        ct_own[i] = nn(hot[i * quarter:(i + 1) * quarter, :], cot[:, own_cols])
    at_end = jnp.logical_or(c == 0, c == far_end)

    def ct_step(where, d):
        @pl.when(where)
        def _():
            for piece in range(4):
                line(d, piece, *ct)

    pl.semaphore_wait(barrier, C - 1 + len(peers))
    ct_step(at_end, near)
    tables[:, :three] = nn(table[...], wqkv[...]).astype(BF16)
    tables[:, three:] = table[:, own_cols]

    def project(i, carry):
        at = pl.ds(pl.multiple_of(i * 256, 256), 256)
        proj[at, :] = contract_rows(hot[:, at], tables[...]).astype(BF16)
        return carry

    lax.fori_loop(0, tok // 256, project, 0)

    kv_own[...] = jnp.zeros_like(kv_own)

    def qkv(b, head):
        at = pl.ds(pl.multiple_of(b * BLOCK, BLOCK), BLOCK)
        base = head * 3 * dh
        return (proj[at, base:base + dh], proj[at, base + dh:base + 2 * dh],
                proj[at, base + 2 * dh:base + 3 * dh])

    def key_values(b, carry):
        for head in range(heads):
            _, k, v = qkv(b, head)
            kv_loc[b, head] = kv_own[head]
            kv_own[head] = kv_own[head] + contract_rows(k, v)
        return carry

    lax.fori_loop(0, blocks, key_values, 0)


    def kv_step(place):
        @pl.when(c == place)
        def _():
            for head in range(heads):
                line(0, head, *kv)

    kv_step(0)

    def wo_copy(n):
        return remote(wo_send.at[peers[n]], wo_recv.at[h], wo_ss.at[n], wo_rs.at[n], c, peers[n])

    for block in range(4):
        wo_send[block] = wout[:, block * cols:(block + 1) * cols].astype(F32)
    for n in range(3):
        wo_copy(n).start()

    def cotangent(i, carry):
        at = pl.ds(pl.multiple_of(i * 256, 256), 256)
        gattn[at, :] = contract_cols(cot[at, :], wout[...])
        return carry

    lax.fori_loop(0, tok // 256, cotangent, 0)
    kv_step(1)

    mask = lower_mask(BLOCK)

    def score(b, carry):
        for head in range(heads):
            q, k, _ = qkv(b, head)
            scores[b, head] = jnp.where(mask, contract_cols(q, k), 0.0).astype(BF16)
        return carry

    lax.fori_loop(0, blocks, score, 0)
    kv_step(2)

    per = vocab // CHUNKS
    for place in range(3, C):
        kv_step(place)
    ct_step(jnp.logical_not(at_end), near)

    qg_own[...] = jnp.zeros_like(qg_own)
    gn_own[...] = jnp.zeros_like(gn_own)
    for head in range(heads):
        kv_own[head] = init[head] + kv_recv[0, head]

    def forward(b, carry):
        at = pl.ds(pl.multiple_of(b * BLOCK, BLOCK), BLOCK)
        for head in range(heads):
            q, k, v = qkv(b, head)
            mine = slice(head * dh, (head + 1) * dh)
            state = kv_loc[b, head] + kv_own[head]
            kv_loc[b, head] = state
            high, low = split(state)
            raw = nn(q, high) + nn(q, low) + nn(scores[b, head], v)
            inv = lax.rsqrt(jnp.mean(raw * raw, axis=-1, keepdims=True) + EPS)
            normed = raw * inv
            g_row = gain[head:head + 1, :]
            attn = (normed * g_row).astype(BF16)
            attn_bf[at, mine] = attn
            attn_send[at, mine] = attn.astype(F32)
            ga = gattn[at, mine]
            gn_own[0, head:head + 1, :] += jnp.sum(ga * normed, axis=0, keepdims=True)
            dn = ga * g_row
            g = inv * (dn - normed * jnp.mean(dn * normed, axis=-1, keepdims=True))
            g = g.astype(BF16)
            grad_bf[at, mine] = g
            outer = contract_rows(q, g)
            qg_loc[b, head] = outer
            qg_own[head] += outer
        return carry

    half = blocks // 2
    lax.fori_loop(0, half, forward, 0)
    ct_step(jnp.logical_not(at_end), 1 - near)
    lax.fori_loop(half, blocks, forward, 0)

    at_sib = remote(attn_send, attn_recv.at[h], at_ss.at[0], at_rs.at[0], c, sib)
    at_across = remote(attn_send, attn_recv.at[h], at_ss.at[1], at_rs.at[1], c, across)
    at_relay = remote(attn_recv.at[across], attn_recv.at[across], at_ss.at[2], at_rs.at[2], c, sib)

    def qg_step(where, d):
        @pl.when(where)
        def _():
            for piece in range(heads):
                line(d, piece, *qg)
            line(d, 0, *gn)

    qg_step(at_end, near)
    at_sib.start()
    at_across.start()

    def weight(i, carry):
        gw_own[i] = contract_rows(
            attn_bf[...], cot[:, pl.ds(pl.multiple_of(i * cols, cols), cols)])
        return carry

    lax.fori_loop(0, C, weight, 0)

    near_place = jnp.where(near == 0, c, far_end - c)

    def gw_to(k):
        place = k + jnp.where(k >= near_place, 1, 0)
        return jnp.where(near == 0, place, far_end - place)

    def gw_copy(to):
        return remote(gw_own.at[to], gw_recv.at[c], gw_ss.at[to], gw_rs.at[c], to, h)

    def gw_start(k):
        gw_copy(gw_to(k)).start()

    gw_start(0)
    qg_step(jnp.logical_not(at_end), near)

    def backward(b, carry):
        at = pl.ds(pl.multiple_of(b * BLOCK, BLOCK), BLOCK)
        for head in range(heads):
            q, k, v = qkv(b, head)
            base = head * 3 * dh
            g = grad_bf[at, head * dh:(head + 1) * dh]
            high, low = split(kv_loc[b, head])
            gs = jnp.where(mask, contract_cols(g, v), 0.0).astype(BF16)
            dq = contract_cols(g, high) + contract_cols(g, low) + nn(gs, k)
            gproj[at, base:base + dh] = dq.astype(BF16)
            local_kv[at, head * 2 * dh:head * 2 * dh + dh] = contract_rows(gs, q)
            local_kv[at, head * 2 * dh + dh:(head + 1) * 2 * dh] = contract_rows(scores[b, head], g)
        return carry

    lax.fori_loop(0, half, backward, 0)
    qg_step(jnp.logical_not(at_end), 1 - near)
    lax.fori_loop(half, blocks, backward, 0)
    qg_step(at_end, 1 - near)

    gw_start(1)

    for head in range(heads):
        grad_init[head] = qg_own[head] + (qg_recv[0, head] + qg_recv[1, head])
    grad_gain[...] = (gn_own[0] + (gn_recv[0, 0] + gn_recv[1, 0]))[:heads, :]
    for head in range(heads):
        kv_own[head] = qg_recv[1, head]

    def later(step, carry):
        b = blocks - 1 - step
        at = pl.ds(pl.multiple_of(b * BLOCK, BLOCK), BLOCK)
        for head in range(heads):
            _, k, v = qkv(b, head)
            base = head * 3 * dh
            after = kv_own[head]
            high, low = split(after)
            kv_own[head] = after + qg_loc[b, head]
            dk = local_kv[at, head * 2 * dh:head * 2 * dh + dh]
            dv = local_kv[at, head * 2 * dh + dh:(head + 1) * 2 * dh]
            dk = dk + contract_cols(v, high) + contract_cols(v, low)
            dv = dv + nn(k, high) + nn(k, low)
            gproj[at, base + dh:base + 2 * dh] = dk.astype(BF16)
            gproj[at, base + 2 * dh:base + 3 * dh] = dv.astype(BF16)
        return carry

    lax.fori_loop(0, blocks, later, 0)

    for i in range(CHUNKS):
        voc_own[i] = nn(hot[i * per:(i + 1) * per, :], gproj[...])

        @pl.when(at_end)
        def _():
            line(near, i, *voc)

    ct_step(at_end, 1 - near)

    half_rows = per // 2
    my_half = pl.ds(pl.multiple_of(core * half_rows, half_rows), half_rows)
    sib_half = pl.ds(pl.multiple_of((1 - core) * half_rows, half_rows), half_rows)

    def core_copy(i):
        return remote(head_part.at[i, sib_half, :], core_recv.at[i],
                      tab_ss.at[0, i], tab_rs.at[0, i], c, sib)

    def cross_copy(i):
        return remote(pair_sum.at[i], cross_recv.at[i], tab_ss.at[1, i], tab_rs.at[1, i], c, across)

    def final_copy(i):
        rows = pl.ds(pl.multiple_of(i * per + core * half_rows, half_rows), half_rows)
        return remote(grad_table.at[rows, :], grad_table.at[rows, :],
                      tab_ss.at[2, i], tab_rs.at[2, i], c, sib)

    def start_head(i):
        total = voc_own[i] + (voc_recv[0, i] + voc_recv[1, i])
        voc_own[i] = total
        both = contract_cols(jnp.concatenate(split(total), axis=0), wqkv[...])
        head_part[i] = both[:per] + both[per:]
        piece, off = i * per // quarter, i * per % quarter
        rows = slice(off, off + per)
        cot_sum = ct_own[piece, rows, :] + (ct_recv[0, piece, rows, :] + ct_recv[1, piece, rows, :])
        head_part[i, :, own_cols] = head_part[i, :, own_cols] + cot_sum
        core_copy(i).start()

    def start_cross(i):
        core_copy(i).wait_recv()
        pair_sum[i] = head_part[i, my_half, :] + core_recv[i]
        cross_copy(i).start()

    def start_final(i):
        cross_copy(i).wait_recv()
        rows = pl.ds(pl.multiple_of(i * per + core * half_rows, half_rows), half_rows)
        grad_table[rows, :] = pair_sum[i] + cross_recv[i]
        final_copy(i).start()

    def out_rows(i):
        at = slice(i * (tok // 4), (i + 1) * (tok // 4))
        mixed = nn(attn_bf[at, :], wo_recv[h].astype(BF16))
        for peer in peers:
            mixed = mixed + nn(attn_recv[peer, at, :].astype(BF16), wo_recv[peer].astype(BF16))
        layer_out[at, :] = (proj[at, three:].astype(F32) + mixed).astype(BF16)

    wo_recv[h] = wout[:, own_cols].astype(F32)

    for i in range(CHUNKS + 1):
        if i < CHUNKS:
            @pl.when(jnp.logical_not(at_end))
            def _():
                line(near, i, *voc)
        if i == 2:
            at_across.wait_recv()
            at_relay.start()
        if i > 0:
            line(1 - near, i - 1, *voc)
            start_head(i - 1)
            if i > 1:
                start_cross(i - 2)
            if i > 2:
                start_final(i - 3)
        if i == 3:
            at_sib.wait_recv()
            at_relay.wait_recv()
            for n in range(3):
                remote(wo_send.at[peers[n]], wo_recv.at[peers[n]], wo_ss.at[n], wo_rs.at[n],
                       c, peers[n]).wait_recv()
        if 3 <= i < 7:
            out_rows(i - 3)

    gw_start(2)
    start_cross(CHUNKS - 1)
    start_final(CHUNKS - 2)

    rows = pl.ds(pl.multiple_of(c * (width // C), width // C), width // C)
    total_w = voc_own[...].reshape(vocab, three)
    high, low = split(total_w)
    grad_wqkv[...] = contract_rows(table[:, rows], high) + contract_rows(table[:, rows], low)
    start_final(CHUNKS - 1)

    gw_recv[c] = gw_own[c]
    for step in range(1, C):
        source = lax.rem(c + step, C)
        remote(gw_own.at[source], gw_recv.at[source], gw_ss.at[source], gw_rs.at[source],
               source, h).wait_recv()
    grad_wout[...] = (gw_recv[0] + gw_recv[1]) + (gw_recv[2] + gw_recv[3])

    for i in range(CHUNKS):
        other = pl.ds(pl.multiple_of(i * per + (1 - core) * half_rows, half_rows), half_rows)
        remote(grad_table.at[other, :], grad_table.at[other, :],
               tab_ss.at[2, i], tab_rs.at[2, i], c, sib).wait_recv()
        core_copy(i).wait_send()
        cross_copy(i).wait_send()
        final_copy(i).wait_send()
        for d in range(2):
            line_sent(d, i, *voc[1:])
    for head in range(heads):
        line_sent(0, head, *kv[1:])
    for d in range(2):
        for piece in range(heads):
            line_sent(d, piece, *qg[1:])
        line_sent(d, 0, *gn[1:])
        for piece in range(4):
            line_sent(d, piece, *ct[1:])
    for n in range(3):
        wo_copy(n).wait_send()
    for k in range(C - 1):
        gw_copy(gw_to(k)).wait_send()
    at_sib.wait_send()
    at_across.wait_send()
    at_relay.wait_send()


def hand_over(*refs):
    sems = refs[12]
    copies = [pltpu.make_async_copy(refs[i], refs[i + 6], sems.at[i]) for i in range(6)]
    for copy in copies:
        copy.start()
    for copy in copies:
        copy.wait()


def one_kernel(event_ids, embed_table, w_qkv, norm_gain, w_out, init_state, out_grad):
    tok, = event_ids.shape
    vocab, width = embed_table.shape
    heads, dh, _ = init_state.shape
    C = lax.axis_size("ctx")
    cols = heads * dh
    three = 3 * cols
    blocks = tok // BLOCK
    per = vocab // CHUNKS
    vmem = lambda *shape: pltpu.VMEM(shape, F32)
    half = lambda *shape: pltpu.VMEM(shape, BF16)
    dma = lambda *shape: pltpu.SemaphoreType.DMA(shape)
    shapes = [
        half(vocab, tok), half(vocab, three + cols), half(tok, three + cols), half(tok, three),
        half(blocks, heads, BLOCK, BLOCK), vmem(blocks, heads, dh, dh), vmem(blocks, heads, dh, dh),
        vmem(tok, cols), vmem(tok, 2 * cols), half(tok, cols), half(tok, cols),
        vmem(heads, dh, dh), vmem(1, heads, dh, dh), vmem(1, heads, dh, dh),
        vmem(heads, dh, dh), vmem(2, heads, dh, dh), vmem(2, heads, dh, dh),
        vmem(1, 8, dh), vmem(2, 1, 8, dh), vmem(2, 1, 8, dh),
        vmem(4, vocab // 4, cols), vmem(2, 4, vocab // 4, cols), vmem(2, 4, vocab // 4, cols),
        vmem(4, cols, cols), vmem(4, cols, cols), vmem(tok, cols), vmem(4, tok, cols),
        vmem(C, cols, width // C), vmem(C, cols, width // C),
        vmem(CHUNKS, per, three), vmem(2, CHUNKS, per, three), vmem(2, CHUNKS, per, three),
        vmem(CHUNKS, per, width), vmem(CHUNKS, per // 2, width), vmem(CHUNKS, per // 2, width),
        vmem(CHUNKS, per // 2, width),
        dma(1, heads), dma(1, heads), dma(2, heads), dma(2, heads),
        dma(2, 1), dma(2, 1), dma(2, 4), dma(2, 4), dma(3), dma(3),
        dma(3), dma(3), dma(C), dma(C), dma(2, CHUNKS), dma(2, CHUNKS),
        dma(3, CHUNKS), dma(3, CHUNKS),
    ]
    outs = pl.pallas_call(
        functools.partial(layer_kernel, (C, tok, vocab, width, heads, dh)),
        out_shape=(
            jax.ShapeDtypeStruct((tok, cols), BF16),
            jax.ShapeDtypeStruct((width // C, three), F32),
            jax.ShapeDtypeStruct((cols, width // C), F32),
            jax.ShapeDtypeStruct((heads, dh), F32),
            jax.ShapeDtypeStruct((heads, dh, dh), F32),
            jax.ShapeDtypeStruct((vocab, width), F32),
        ),
        in_specs=[pl.BlockSpec(memory_space=pltpu.VMEM)] * 7,
        out_specs=(pl.BlockSpec(memory_space=pltpu.VMEM),) * 6,
        scratch_shapes=shapes,
        compiler_params=pltpu.CompilerParams(
            collective_id=0, has_side_effects=True, vmem_limit_bytes=56 * 1024 * 1024
        ),
    )(event_ids.reshape(1, tok), embed_table, w_qkv, norm_gain.reshape(heads, dh), w_out,
      init_state, out_grad)
    outs = pl.pallas_call(
        hand_over,
        out_shape=tuple(jax.ShapeDtypeStruct(out.shape, out.dtype) for out in outs),
        in_specs=[pl.BlockSpec(memory_space=pl.ANY)] * 6,
        out_specs=(pl.BlockSpec(memory_space=pl.ANY),) * 6,
        scratch_shapes=[pltpu.SemaphoreType.DMA((6,))],
    )(*outs)
    layer_out, grad_wqkv, grad_wout, grad_gain, grad_init, grad_table = outs
    return layer_out, grad_wqkv, grad_wout, grad_gain.reshape(cols), grad_init, grad_table


def solution(mesh):
    in_specs = (
        P(("parts", "ctx")),
        P(),
        P(None, "head"),
        P("head"),
        P("head", None),
        P("head", None, None),
        P(("parts", "ctx"), None),
    )
    out_specs = (
        P(("parts", "ctx"), "head"),
        P(("parts", "ctx"), "head"),
        P(("parts", "head"), "ctx"),
        P(("parts", "head")),
        P(("parts", "head"), None, None),
        P("parts", None),
    )
    fits = mesh.shape["ctx"] == 4 and mesh.shape["head"] == 4
    return jax.shard_map(
        one_kernel if fits else per_device, mesh=mesh, in_specs=in_specs, out_specs=out_specs, check_vma=False
    )
```

```python
import functools
import jax
import jax.numpy as jnp
from jax import lax
from jax.experimental import pallas as pl
from jax.experimental.pallas import tpu as pltpu
from jax.sharding import PartitionSpec as P

BLOCK = 128


EPS = 1e-05


def prefix(part, axis, combine, identity, reverse):
    count = lax.axis_size(axis)
    place = lax.axis_index(axis)
    ahead = count - 1 - place if reverse else place
    gathered = lax.all_gather(part, axis)
    state = jnp.zeros_like(part) + jnp.asarray(identity, part.dtype)

    def one(step, state):
        source = count - 1 - step if reverse else step
        return combine(state, lax.dynamic_index_in_dim(gathered, source, 0, False))

    return lax.fori_loop(0, ahead, one, state)


def lower_mask(block_len):
    rows_idx = lax.broadcasted_iota(jnp.int32, (block_len, block_len), 0)
    cols_idx = lax.broadcasted_iota(jnp.int32, (block_len, block_len), 1)
    return rows_idx >= cols_idx


def add_states(earlier, later_one):
    return earlier + later_one


def contract_rows(left, right):
    return lax.dot_general(
        left, right, (((0,), (0,)), ((), ())), preferred_element_type=jnp.float32
    )


def contract_cols(left, right):
    return lax.dot_general(
        left, right, (((1,), (1,)), ((), ())), preferred_element_type=jnp.float32
    )


def per_device(event_ids, embed_table, w_qkv, norm_gain, w_out, init_state, out_grad):
    highest = lax.Precision.HIGHEST
    tok_rows = event_ids.shape[0]
    vocab_size = embed_table.shape[0]
    head_local = init_state.shape[0]
    head_dim = init_state.shape[1]
    block_len = BLOCK
    blocks = tok_rows // block_len
    one_hot = event_ids[:, None] == lax.broadcasted_iota(jnp.int32, (1, vocab_size), 1)
    embedded = jnp.dot(
        one_hot.astype(jnp.bfloat16), embed_table, preferred_element_type=jnp.float32
    ).astype(jnp.bfloat16)
    projected = jnp.dot(embedded, w_qkv, preferred_element_type=jnp.float32).astype(jnp.bfloat16)
    shaped = projected.reshape(blocks, block_len, head_local, 3, head_dim)
    queries = shaped[:, :, :, 0]
    key_rows = shaped[:, :, :, 1]
    value_rows = shaped[:, :, :, 2]
    block_kv = jnp.einsum(
        "bshd,bshe->bhde", key_rows, value_rows, preferred_element_type=jnp.float32
    )
    own_total = jnp.sum(block_kv, axis=0)
    zero_state = jnp.zeros_like(own_total)
    earlier_state = prefix(own_total, "ctx", add_states, zero_state, False)
    cumulative = jnp.cumsum(block_kv, axis=0)
    shifted = jnp.concatenate([jnp.zeros_like(block_kv[:1]), cumulative[:-1]], axis=0)
    states = init_state[None] + earlier_state[None] + shifted
    mask_tri = lower_mask(block_len)[None, None]
    scores = jnp.einsum("bthd,bshd->bhts", queries, key_rows, preferred_element_type=jnp.float32)
    scores_bf = jnp.where(mask_tri, scores, 0.0).astype(jnp.bfloat16)
    inter = jnp.einsum("bthd,bhde->bthe", queries.astype(jnp.float32), states, precision=highest)
    intra = jnp.einsum("bhts,bshe->bthe", scores_bf, value_rows, preferred_element_type=jnp.float32)
    raw_out = inter + intra
    inv_rms = lax.rsqrt(jnp.mean(raw_out * raw_out, axis=-1, keepdims=True) + EPS)
    normed = raw_out * inv_rms
    gain_view = norm_gain.reshape(head_local, head_dim)
    attn = (normed * gain_view).astype(jnp.bfloat16).reshape(tok_rows, head_local * head_dim)
    head_terms = jnp.dot(attn, w_out, preferred_element_type=jnp.float32)
    mixed = lax.psum_scatter(head_terms, "head", scatter_dimension=1, tiled=True)
    out_cols = mixed.shape[1]
    residual = lax.dynamic_slice_in_dim(embedded, lax.axis_index("head") * out_cols, out_cols, 1)
    layer_out = (residual.astype(jnp.float32) + mixed).astype(jnp.bfloat16)
    grad_attn = contract_cols(out_grad, w_out)
    grad_wout_local = contract_rows(attn, out_grad)
    normed_flat = normed.reshape(tok_rows, head_local * head_dim)
    grad_gain_local = jnp.sum(grad_attn * normed_flat, axis=0)
    grad_norm = (grad_attn * norm_gain).reshape(blocks, block_len, head_local, head_dim)
    grad_raw = inv_rms * (grad_norm - normed * jnp.mean(grad_norm * normed, axis=-1, keepdims=True))
    grad_bf = grad_raw.astype(jnp.bfloat16)
    grad_scores = jnp.einsum(
        "bthe,bshe->bhts", grad_bf, value_rows, preferred_element_type=jnp.float32
    )
    grad_scores = jnp.where(mask_tri, grad_scores, 0.0).astype(jnp.bfloat16)
    block_qg = jnp.einsum("bthd,bthe->bhde", queries, grad_bf, preferred_element_type=jnp.float32)
    own_grad = jnp.sum(block_qg, axis=0)
    later_state = prefix(own_grad, "ctx", add_states, zero_state, True)
    reversed_sum = jnp.cumsum(block_qg[::-1], axis=0)[::-1]
    local_after = jnp.concatenate([reversed_sum[1:], jnp.zeros_like(block_qg[:1])], axis=0)
    after = later_state[None] + local_after
    grad_q = jnp.einsum(
        "bthe,bhde->bthd", grad_bf.astype(jnp.float32), states, precision=highest
    ) + jnp.einsum("bhts,bshd->bthd", grad_scores, key_rows, preferred_element_type=jnp.float32)
    grad_k = jnp.einsum(
        "bshe,bhde->bshd", value_rows.astype(jnp.float32), after, precision=highest
    ) + jnp.einsum("bhts,bthd->bshd", grad_scores, queries, preferred_element_type=jnp.float32)
    grad_v = jnp.einsum(
        "bshd,bhde->bshe", key_rows.astype(jnp.float32), after, precision=highest
    ) + jnp.einsum("bhts,bthe->bshe", scores_bf, grad_bf, preferred_element_type=jnp.float32)
    grad_proj = (
        jnp.stack([grad_q, grad_k, grad_v], axis=3)
        .astype(jnp.bfloat16)
        .reshape(tok_rows, head_local * 3 * head_dim)
    )
    vocab_proj = contract_rows(one_hot.astype(jnp.bfloat16), grad_proj)
    vocab_cot = contract_rows(one_hot.astype(jnp.bfloat16), out_grad)
    summed_vocab, summed_wout, summed_gain, grad_init, summed_cot = lax.psum(
        (vocab_proj, grad_wout_local, grad_gain_local, own_grad, vocab_cot), "ctx"
    )
    summed_wqkv = lax.dot_general(
        embed_table.astype(jnp.float32),
        summed_vocab,
        (((0,), (0,)), ((), ())),
        precision=highest,
        preferred_element_type=jnp.float32,
    )
    head_table = lax.dot_general(
        summed_vocab,
        w_qkv.astype(jnp.float32),
        (((1,), (1,)), ((), ())),
        precision=highest,
        preferred_element_type=jnp.float32,
    )
    grad_table = lax.psum(head_table, "head") + summed_cot
    ctx_pos = lax.axis_index("ctx")
    width_rows = summed_wqkv.shape[0] // lax.axis_size("ctx")
    own_wqkv = lax.dynamic_slice_in_dim(summed_wqkv, ctx_pos * width_rows, width_rows, 0)
    own_wout = lax.dynamic_slice_in_dim(summed_wout, ctx_pos * width_rows, width_rows, 1)
    return (layer_out, own_wqkv, own_wout, summed_gain, grad_init, grad_table)


F32 = jnp.float32
BF16 = jnp.bfloat16
CHUNKS = 8
GW_AT = 5


def nn(left, right):
    return lax.dot_general(left, right, (((1,), (0,)), ((), ())), preferred_element_type=F32)


def split(value):
    high = value.astype(BF16)
    return high, (value - high.astype(F32)).astype(BF16)


def layer_kernel(
    dims,
    ids, table, wqkv, gain, wout, init, cot,
    layer_out, grad_wqkv, grad_wout, grad_gain, grad_init, grad_table,
    hot, tables, proj, gproj, scores, kv_loc, qg_loc, gattn, local_kv, grad_bf, attn_bf,
    kv_own, kv_recv, kv_stage, qg_own, qg_recv, qg_stage, gn_own, gn_recv, gn_stage, ct_own, ct_recv, ct_stage,
    wo_send, wo_recv, attn_send, attn_recv, gw_own, gw_recv, gw_stage,
    voc_own, voc_recv, voc_stage, head_part, core_recv, pair_sum, cross_recv,
    kv_ss, kv_rs, qg_ss, qg_rs, gn_ss, gn_rs, ct_ss, ct_rs, wo_ss, wo_rs, at_ss, at_rs, gw_ss, gw_rs,
    voc_ss, voc_rs, tab_ss, tab_rs,
):
    C, tok, vocab, width, heads, dh = dims
    blocks = tok // BLOCK
    cols = heads * dh
    three = 3 * cols
    part = lax.axis_index("parts")
    c = lax.axis_index("ctx")
    h = lax.axis_index("head")
    core = lax.rem(h, 2)
    sib = h + 1 - 2 * core
    across = lax.rem(h + 2, 4)
    diag = lax.rem(sib + 2, 4)
    peers = (sib, across, diag)
    far_end = C - 1
    near = c // (C // 2)
    own_cols = pl.ds(pl.multiple_of(h * cols, cols), cols)

    def remote(src, dst, ss, rs, ctx_to, head_to):
        return pltpu.make_async_remote_copy(
            src_ref=src, dst_ref=dst, send_sem=ss, recv_sem=rs,
            device_id=(part, ctx_to, head_to), device_id_type=pl.DeviceIdType.MESH,
        )

    barrier = pltpu.get_barrier_semaphore()
    for step in range(1, C):
        pl.semaphore_signal(barrier, inc=1, device_id=(part, lax.rem(c + step, C), h),
                            device_id_type=pl.DeviceIdType.MESH)
    for peer in peers:
        pl.semaphore_signal(barrier, inc=1, device_id=(part, c, peer),
                            device_id_type=pl.DeviceIdType.MESH)

    def has_recv(d):
        return jnp.where(d == 0, c > 0, c < far_end)

    def has_send(d):
        return jnp.where(d == 0, c < far_end, c > 0)

    def line_copy(d, i, recv, stage, ss, rs):
        to = jnp.clip(c + 1 - 2 * d, 0, far_end)
        return remote(stage.at[d, i], recv.at[d, i], ss.at[d, i], rs.at[d, i], to, h)

    def line(d, i, own, recv, stage, ss, rs):
        @pl.when(has_recv(d))
        def _():
            line_copy(d, i, recv, stage, ss, rs).wait_recv()

        @pl.when(jnp.logical_not(has_recv(d)))
        def _():
            recv[d, i] = jnp.zeros(recv.shape[2:], F32)

        @pl.when(has_send(d))
        def _():
            stage[d, i] = own[i] + recv[d, i]
            line_copy(d, i, recv, stage, ss, rs).start()

    def line_sent(d, i, recv, stage, ss, rs):
        @pl.when(has_send(d))
        def _():
            line_copy(d, i, recv, stage, ss, rs).wait_send()

    kv = (kv_own, kv_recv, kv_stage, kv_ss, kv_rs)
    qg = (qg_own, qg_recv, qg_stage, qg_ss, qg_rs)
    gn = (gn_own, gn_recv, gn_stage, gn_ss, gn_rs)
    ct = (ct_own, ct_recv, ct_stage, ct_ss, ct_rs)
    voc = (voc_own, voc_recv, voc_stage, voc_ss, voc_rs)

    hot[...] = (lax.broadcasted_iota(jnp.int32, (vocab, tok), 0) == ids[...]).astype(BF16)
    quarter = vocab // 4
    for i in range(4):
        ct_own[i] = nn(hot[i * quarter:(i + 1) * quarter, :], cot[:, own_cols])
    at_end = jnp.logical_or(c == 0, c == far_end)

    def ct_step(where, d):
        @pl.when(where)
        def _():
            for piece in range(4):
                line(d, piece, *ct)

    pl.semaphore_wait(barrier, C - 1 + len(peers))
    ct_step(at_end, near)
    tables[:, :three] = nn(table[...], wqkv[...]).astype(BF16)
    tables[:, three:] = table[:, own_cols]

    def project(i, carry):
        at = pl.ds(pl.multiple_of(i * 256, 256), 256)
        proj[at, :] = contract_rows(hot[:, at], tables[...]).astype(BF16)
        return carry

    lax.fori_loop(0, tok // 256, project, 0)

    kv_own[...] = jnp.zeros_like(kv_own)

    def qkv(b, head):
        at = pl.ds(pl.multiple_of(b * BLOCK, BLOCK), BLOCK)
        base = head * 3 * dh
        return (proj[at, base:base + dh], proj[at, base + dh:base + 2 * dh],
                proj[at, base + 2 * dh:base + 3 * dh])

    def key_values(b, carry):
        for head in range(heads):
            _, k, v = qkv(b, head)
            kv_loc[b, head] = kv_own[head]
            kv_own[head] = kv_own[head] + contract_rows(k, v)
        return carry

    lax.fori_loop(0, blocks, key_values, 0)


    def kv_step(place):
        @pl.when(c == place)
        def _():
            for head in range(heads):
                line(0, head, *kv)

    kv_step(0)

    def wo_copy(n):
        return remote(wo_send.at[peers[n]], wo_recv.at[h], wo_ss.at[n], wo_rs.at[n], c, peers[n])

    for block in range(4):
        wo_send[block] = wout[:, block * cols:(block + 1) * cols].astype(F32)
    for n in range(3):
        wo_copy(n).start()

    def cotangent(i, carry):
        at = pl.ds(pl.multiple_of(i * 256, 256), 256)
        gattn[at, :] = contract_cols(cot[at, :], wout[...])
        return carry

    lax.fori_loop(0, tok // 256, cotangent, 0)
    kv_step(1)

    mask = lower_mask(BLOCK)

    def score(b, carry):
        for head in range(heads):
            q, k, _ = qkv(b, head)
            scores[b, head] = jnp.where(mask, contract_cols(q, k), 0.0).astype(BF16)
        return carry

    lax.fori_loop(0, blocks, score, 0)
    kv_step(2)

    per = vocab // CHUNKS
    for place in range(3, C):
        kv_step(place)
    ct_step(jnp.logical_not(at_end), near)

    qg_own[...] = jnp.zeros_like(qg_own)
    gn_own[...] = jnp.zeros_like(gn_own)
    for head in range(heads):
        kv_own[head] = init[head] + kv_recv[0, head]

    def forward(b, carry):
        at = pl.ds(pl.multiple_of(b * BLOCK, BLOCK), BLOCK)
        for head in range(heads):
            q, k, v = qkv(b, head)
            mine = slice(head * dh, (head + 1) * dh)
            state = kv_loc[b, head] + kv_own[head]
            kv_loc[b, head] = state
            high, low = split(state)
            raw = nn(q, high) + nn(q, low) + nn(scores[b, head], v)
            inv = lax.rsqrt(jnp.mean(raw * raw, axis=-1, keepdims=True) + EPS)
            normed = raw * inv
            g_row = gain[head:head + 1, :]
            attn = (normed * g_row).astype(BF16)
            attn_bf[at, mine] = attn
            attn_send[at, mine] = attn.astype(F32)
            ga = gattn[at, mine]
            gn_own[0, head:head + 1, :] += jnp.sum(ga * normed, axis=0, keepdims=True)
            dn = ga * g_row
            g = inv * (dn - normed * jnp.mean(dn * normed, axis=-1, keepdims=True))
            g = g.astype(BF16)
            grad_bf[at, mine] = g
            outer = contract_rows(q, g)
            qg_loc[b, head] = outer
            qg_own[head] += outer
        return carry

    half = blocks // 2
    lax.fori_loop(0, half, forward, 0)
    ct_step(jnp.logical_not(at_end), 1 - near)
    lax.fori_loop(half, blocks, forward, 0)

    at_sib = remote(attn_send, attn_recv.at[h], at_ss.at[0], at_rs.at[0], c, sib)
    at_across = remote(attn_send, attn_recv.at[h], at_ss.at[1], at_rs.at[1], c, across)
    at_relay = remote(attn_recv.at[across], attn_recv.at[across], at_ss.at[2], at_rs.at[2], c, sib)

    def qg_step(where, d):
        @pl.when(where)
        def _():
            for piece in range(heads):
                line(d, piece, *qg)
            line(d, 0, *gn)

    qg_step(at_end, near)
    at_sib.start()
    at_across.start()

    def weight(i, carry):
        gw_own[i] = contract_rows(
            attn_bf[...], cot[:, pl.ds(pl.multiple_of(i * cols, cols), cols)])
        return carry

    lax.fori_loop(0, C, weight, 0)

    def gw_block(place):
        return jnp.where(near == 0, place, far_end - place)

    def gw_copy(d, place, source):
        block = gw_block(place)
        to = jnp.clip(c + 1 - 2 * d, 0, far_end)
        return remote(source.at[d, block] if source is gw_stage else source.at[block],
                      gw_recv.at[d, block], gw_ss.at[d, block], gw_rs.at[d, block], to, h)

    def gw_pass(d, place):
        block = gw_block(place)
        gw_copy(d, place, gw_stage).wait_recv()
        gw_stage[d, block] = gw_own[block] + gw_recv[d, block]
        gw_copy(d, place, gw_stage).start()

    @pl.when(at_end)
    def _():
        for place in range(C - 1, 1, -1):
            gw_copy(near, place, gw_own).start()

    qg_step(jnp.logical_not(at_end), near)

    def backward(b, carry):
        at = pl.ds(pl.multiple_of(b * BLOCK, BLOCK), BLOCK)
        for head in range(heads):
            q, k, v = qkv(b, head)
            base = head * 3 * dh
            g = grad_bf[at, head * dh:(head + 1) * dh]
            high, low = split(kv_loc[b, head])
            gs = jnp.where(mask, contract_cols(g, v), 0.0).astype(BF16)
            dq = contract_cols(g, high) + contract_cols(g, low) + nn(gs, k)
            gproj[at, base:base + dh] = dq.astype(BF16)
            local_kv[at, head * 2 * dh:head * 2 * dh + dh] = contract_rows(gs, q)
            local_kv[at, head * 2 * dh + dh:(head + 1) * 2 * dh] = contract_rows(scores[b, head], g)
        return carry

    lax.fori_loop(0, half, backward, 0)
    qg_step(jnp.logical_not(at_end), 1 - near)
    lax.fori_loop(half, blocks, backward, 0)
    qg_step(at_end, 1 - near)

    for head in range(heads):
        grad_init[head] = qg_own[head] + (qg_recv[0, head] + qg_recv[1, head])
    grad_gain[...] = (gn_own[0] + (gn_recv[0, 0] + gn_recv[1, 0]))[:heads, :]
    for head in range(heads):
        kv_own[head] = qg_recv[1, head]

    def later(step, carry):
        b = blocks - 1 - step
        at = pl.ds(pl.multiple_of(b * BLOCK, BLOCK), BLOCK)
        for head in range(heads):
            _, k, v = qkv(b, head)
            base = head * 3 * dh
            after = kv_own[head]
            high, low = split(after)
            kv_own[head] = after + qg_loc[b, head]
            dk = local_kv[at, head * 2 * dh:head * 2 * dh + dh]
            dv = local_kv[at, head * 2 * dh + dh:(head + 1) * 2 * dh]
            dk = dk + contract_cols(v, high) + contract_cols(v, low)
            dv = dv + nn(k, high) + nn(k, low)
            gproj[at, base + dh:base + 2 * dh] = dk.astype(BF16)
            gproj[at, base + 2 * dh:base + 3 * dh] = dv.astype(BF16)
        return carry

    lax.fori_loop(0, blocks, later, 0)

    for i in range(CHUNKS):
        voc_own[i] = nn(hot[i * per:(i + 1) * per, :], gproj[...])

        @pl.when(at_end)
        def _():
            line(near, i, *voc)

    ct_step(at_end, 1 - near)

    half_rows = per // 2
    my_half = pl.ds(pl.multiple_of(core * half_rows, half_rows), half_rows)
    sib_half = pl.ds(pl.multiple_of((1 - core) * half_rows, half_rows), half_rows)

    def core_copy(i):
        return remote(head_part.at[i, sib_half, :], core_recv.at[i],
                      tab_ss.at[0, i], tab_rs.at[0, i], c, sib)

    def cross_copy(i):
        return remote(pair_sum.at[i], cross_recv.at[i], tab_ss.at[1, i], tab_rs.at[1, i], c, across)

    def final_copy(i):
        rows = pl.ds(pl.multiple_of(i * per + core * half_rows, half_rows), half_rows)
        return remote(grad_table.at[rows, :], grad_table.at[rows, :],
                      tab_ss.at[2, i], tab_rs.at[2, i], c, sib)

    def start_head(i):
        total = voc_own[i] + (voc_recv[0, i] + voc_recv[1, i])
        voc_own[i] = total
        both = contract_cols(jnp.concatenate(split(total), axis=0), wqkv[...])
        head_part[i] = both[:per] + both[per:]
        piece, off = i * per // quarter, i * per % quarter
        rows = slice(off, off + per)
        cot_sum = ct_own[piece, rows, :] + (ct_recv[0, piece, rows, :] + ct_recv[1, piece, rows, :])
        head_part[i, :, own_cols] = head_part[i, :, own_cols] + cot_sum
        core_copy(i).start()

    def start_cross(i):
        core_copy(i).wait_recv()
        pair_sum[i] = head_part[i, my_half, :] + core_recv[i]
        cross_copy(i).start()

    def start_final(i):
        cross_copy(i).wait_recv()
        rows = pl.ds(pl.multiple_of(i * per + core * half_rows, half_rows), half_rows)
        grad_table[rows, :] = pair_sum[i] + cross_recv[i]
        final_copy(i).start()

    def out_rows(i):
        at = slice(i * (tok // 4), (i + 1) * (tok // 4))
        mixed = nn(attn_bf[at, :], wo_recv[h].astype(BF16))
        for peer in peers:
            mixed = mixed + nn(attn_recv[peer, at, :].astype(BF16), wo_recv[peer].astype(BF16))
        layer_out[at, :] = (proj[at, three:].astype(F32) + mixed).astype(BF16)

    wo_recv[h] = wout[:, own_cols].astype(F32)

    @pl.when(jnp.logical_not(at_end))
    def _():
        for place in range(C - 1, 1, -1):
            gw_pass(near, place)

    for i in range(CHUNKS + 1):
        if i < CHUNKS:
            @pl.when(jnp.logical_not(at_end))
            def _():
                line(near, i, *voc)
        if i == 2:
            at_across.wait_recv()
            at_relay.start()
        if i > 0:
            line(1 - near, i - 1, *voc)
            start_head(i - 1)
            if i > 1:
                start_cross(i - 2)
            if i > 2:
                start_final(i - 3)
        if i == GW_AT:
            @pl.when(at_end)
            def _():
                gw_copy(near, 1, gw_own).start()

            @pl.when(jnp.logical_not(at_end))
            def _():
                gw_pass(1 - near, 0)

        if i == 3:
            at_sib.wait_recv()
            at_relay.wait_recv()
            for n in range(3):
                remote(wo_send.at[peers[n]], wo_recv.at[peers[n]], wo_ss.at[n], wo_rs.at[n],
                       c, peers[n]).wait_recv()
        if 3 <= i < 7:
            out_rows(i - 3)

    start_cross(CHUNKS - 1)
    start_final(CHUNKS - 2)

    rows = pl.ds(pl.multiple_of(c * (width // C), width // C), width // C)
    total_w = voc_own[...].reshape(vocab, three)
    high, low = split(total_w)
    grad_wqkv[...] = contract_rows(table[:, rows], high) + contract_rows(table[:, rows], low)
    start_final(CHUNKS - 1)

    grad_wout[...] = gw_own[c]
    for d in range(2):
        @pl.when(has_recv(d))
        def _():
            remote(gw_stage.at[d, c], gw_recv.at[d, c], gw_ss.at[d, c], gw_rs.at[d, c], c, h).wait_recv()
            grad_wout[...] += gw_recv[d, c]

    for i in range(CHUNKS):
        other = pl.ds(pl.multiple_of(i * per + (1 - core) * half_rows, half_rows), half_rows)
        remote(grad_table.at[other, :], grad_table.at[other, :],
               tab_ss.at[2, i], tab_rs.at[2, i], c, sib).wait_recv()
        core_copy(i).wait_send()
        cross_copy(i).wait_send()
        final_copy(i).wait_send()
        for d in range(2):
            line_sent(d, i, *voc[1:])
    for head in range(heads):
        line_sent(0, head, *kv[1:])
    for d in range(2):
        for piece in range(heads):
            line_sent(d, piece, *qg[1:])
        line_sent(d, 0, *gn[1:])
        for piece in range(4):
            line_sent(d, piece, *ct[1:])
    for n in range(3):
        wo_copy(n).wait_send()

    @pl.when(at_end)
    def _():
        for place in range(1, C):
            gw_copy(near, place, gw_own).wait_send()

    @pl.when(jnp.logical_not(at_end))
    def _():
        for place in range(2, C):
            gw_copy(near, place, gw_stage).wait_send()
        gw_copy(1 - near, 0, gw_stage).wait_send()

    at_sib.wait_send()
    at_across.wait_send()
    at_relay.wait_send()


def hand_over(*refs):
    for i in range(6):
        refs[i + 6][...] = refs[i][...]


def one_kernel(event_ids, embed_table, w_qkv, norm_gain, w_out, init_state, out_grad):
    tok, = event_ids.shape
    vocab, width = embed_table.shape
    heads, dh, _ = init_state.shape
    C = lax.axis_size("ctx")
    cols = heads * dh
    three = 3 * cols
    blocks = tok // BLOCK
    per = vocab // CHUNKS
    vmem = lambda *shape: pltpu.VMEM(shape, F32)
    half = lambda *shape: pltpu.VMEM(shape, BF16)
    dma = lambda *shape: pltpu.SemaphoreType.DMA(shape)
    shapes = [
        half(vocab, tok), half(vocab, three + cols), half(tok, three + cols), half(tok, three),
        half(blocks, heads, BLOCK, BLOCK), vmem(blocks, heads, dh, dh), vmem(blocks, heads, dh, dh),
        vmem(tok, cols), vmem(tok, 2 * cols), half(tok, cols), half(tok, cols),
        vmem(heads, dh, dh), vmem(1, heads, dh, dh), vmem(1, heads, dh, dh),
        vmem(heads, dh, dh), vmem(2, heads, dh, dh), vmem(2, heads, dh, dh),
        vmem(1, 8, dh), vmem(2, 1, 8, dh), vmem(2, 1, 8, dh),
        vmem(4, vocab // 4, cols), vmem(2, 4, vocab // 4, cols), vmem(2, 4, vocab // 4, cols),
        vmem(4, cols, cols), vmem(4, cols, cols), vmem(tok, cols), vmem(4, tok, cols),
        vmem(C, cols, width // C), vmem(2, C, cols, width // C), vmem(2, C, cols, width // C),
        vmem(CHUNKS, per, three), vmem(2, CHUNKS, per, three), vmem(2, CHUNKS, per, three),
        vmem(CHUNKS, per, width), vmem(CHUNKS, per // 2, width), vmem(CHUNKS, per // 2, width),
        vmem(CHUNKS, per // 2, width),
        dma(1, heads), dma(1, heads), dma(2, heads), dma(2, heads),
        dma(2, 1), dma(2, 1), dma(2, 4), dma(2, 4), dma(3), dma(3),
        dma(3), dma(3), dma(2, C), dma(2, C), dma(2, CHUNKS), dma(2, CHUNKS),
        dma(3, CHUNKS), dma(3, CHUNKS),
    ]
    outs = pl.pallas_call(
        functools.partial(layer_kernel, (C, tok, vocab, width, heads, dh)),
        out_shape=(
            jax.ShapeDtypeStruct((tok, cols), BF16),
            jax.ShapeDtypeStruct((width // C, three), F32),
            jax.ShapeDtypeStruct((cols, width // C), F32),
            jax.ShapeDtypeStruct((heads, dh), F32),
            jax.ShapeDtypeStruct((heads, dh, dh), F32),
            jax.ShapeDtypeStruct((vocab, width), F32),
        ),
        in_specs=[pl.BlockSpec(memory_space=pltpu.VMEM)] * 7,
        out_specs=(pl.BlockSpec(memory_space=pltpu.VMEM),) * 6,
        scratch_shapes=shapes,
        compiler_params=pltpu.CompilerParams(
            collective_id=0, has_side_effects=True, vmem_limit_bytes=56 * 1024 * 1024
        ),
    )(event_ids.reshape(1, tok), embed_table, w_qkv, norm_gain.reshape(heads, dh), w_out,
      init_state, out_grad)
    outs = pl.pallas_call(
        hand_over,
        out_shape=tuple(jax.ShapeDtypeStruct(out.shape, out.dtype) for out in outs),
        in_specs=[pl.BlockSpec(memory_space=pltpu.VMEM)] * 6,
        out_specs=(pl.BlockSpec(memory_space=pltpu.VMEM),) * 6,
    )(*outs)
    layer_out, grad_wqkv, grad_wout, grad_gain, grad_init, grad_table = outs
    return layer_out, grad_wqkv, grad_wout, grad_gain.reshape(cols), grad_init, grad_table


def solution(mesh):
    in_specs = (
        P(("parts", "ctx")),
        P(),
        P(None, "head"),
        P("head"),
        P("head", None),
        P("head", None, None),
        P(("parts", "ctx"), None),
    )
    out_specs = (
        P(("parts", "ctx"), "head"),
        P(("parts", "ctx"), "head"),
        P(("parts", "head"), "ctx"),
        P(("parts", "head")),
        P(("parts", "head"), None, None),
        P("parts", None),
    )
    fits = mesh.shape["ctx"] == 4 and mesh.shape["head"] == 4
    return jax.shard_map(
        one_kernel if fits else per_device, mesh=mesh, in_specs=in_specs, out_specs=out_specs, check_vma=False
    )
```
